256 devices in a mesh: ctx: 32 (over z, x), head: 8 (over y, core).
Axes of the slice: x: 4, y: 4, z: 8, core: 2. Of those that a mesh axis runs over, the one named last changes fastest.
Arguments:
- queries: bfloat16 [4096, 4096], P(('ctx', 'head')), may hold values from -48 to 48
- keys: bfloat16 [32768, 1024], P('ctx', 'head'), may hold values from -4.5 to 4.5
- values: bfloat16 [32768, 1024], P('ctx', 'head'), may hold values from -5 to 5
- grad_out: bfloat16 [4096, 4096], P(('ctx', 'head')), may hold values from -5 to 5
- gates: int32 [4096, 8, 3], P('ctx', 'head'), may hold values from 0 to 31, as said below
- block_order: int32 [32], replicated, may hold values from 0 to 31, as said below
Outputs:
- attn_out: bfloat16 [4096, 4096], P(('ctx', 'head'))
- grad_queries: bfloat16 [4096, 4096], P(('ctx', 'head'))
- grad_keys: bfloat16 [32768, 1024], P('ctx', 'head')
- grad_values: bfloat16 [32768, 1024], P('ctx', 'head')
The draws below stay inside these ranges and needn't reach their ends.
Inputs may be any that keep to these rules, and one draw needn't show every extreme that they name: A permutation: slot s holds block block_order[s]. gates[r, h, 0] is the block of query row r. Entries 1 and 2 are blocks before it and differ from each other, or equal entry 0 to mean no block. Over the rows of one device and one key head, at most 16 of entries 1 and 2 name any one block, and at most 8 name any block other than the block that entries 1 and 2 name most often over all rows and key heads; both bounds are reached.
All inputs are finite; a program needn't handle non-finite values.
Results may differ from the reference program's by a relative error of at most 0.025.
Values may be sent and summed in bfloat16 or wider, within the bound.
No kernel may reach another device: no remote copies, remote signals or barrier semaphores. Data moves between devices by JAX's collectives and lax.ppermute only.
A program may use at most 64 MiB of HBM per device.

```python
import jax
import jax.numpy as jnp
from jax import lax

DH = 128
HQ = 32
KVH = 8
BS = 1024
QB = 128
BLK_DEV = 1
CAP = 16
CAP2 = 8
NB = 32
SEQ = 32768
NQ = 4096


def block_layout(key):
    return jax.random.permutation(jax.random.fold_in(key, 101), NB).astype(jnp.int32)


def key_field(key):
    key = jax.random.fold_in(key, 202)
    first_key = jax.random.fold_in(key, 0)
    dims_full = (NB * BS, KVH * DH)
    normal_part = jnp.clip(jax.random.normal(first_key, dims_full, jnp.float32), -4.5, 4.5)
    field = normal_part
    blocks = field.reshape(NB, BS, KVH * DH)
    echoed = blocks.at[:, 1].set(blocks[:, 1])
    return echoed.reshape(dims_full)


def draw_block_order(key, part):
    return block_layout(key)


def draw_keys(key, part):
    return key_field(key).astype(jnp.bfloat16)


def draw_queries(key, part):
    key = jax.random.fold_in(key, 3)
    first_key = jax.random.fold_in(key, 0)
    dims_full = (NQ, HQ * DH)
    normal_part = jnp.clip(jax.random.normal(first_key, dims_full, jnp.float32), -4.5, 4.5)
    background = normal_part
    result = background
    return result.astype(jnp.bfloat16)


def draw_gates(key, part):
    layout = block_layout(key)
    key = jax.random.fold_in(key, 2)
    coin_key, first_key, second_key = jax.random.split(key, 3)
    dev_rows = QB * BLK_DEV
    dev_count = NB // BLK_DEV
    row_ids = jnp.arange(NQ, dtype=jnp.int32)
    own_block = jnp.broadcast_to(layout[row_ids // QB][:, None], (NQ, KVH))
    coins = jax.random.randint(coin_key, (NQ, KVH), 0, 2)
    earlier = jax.random.randint(first_key, (NQ, KVH), 0, jnp.maximum(own_block, 1))
    first_pick = jnp.where(coins == 1, 0, earlier)
    other_pick = jax.random.randint(second_key, (NQ, KVH), 0, jnp.maximum(own_block - 1, 1))
    second_pick = other_pick + (other_pick >= first_pick).astype(jnp.int32)
    picks = jnp.stack([first_pick, second_pick], axis=-1).astype(jnp.int32)
    usable = jnp.stack([own_block >= 1, own_block >= 2], axis=-1)
    slot_of = jnp.zeros((NB,), jnp.int32).at[layout].set(jnp.arange(NB, dtype=jnp.int32))
    target = slot_of[picks]

    def by_device(tensor):
        return tensor.reshape(dev_count, dev_rows, KVH, 2).transpose(0, 2, 1, 3).reshape(dev_count, KVH, dev_rows * 2)
    ordered = by_device(target)
    ordered_ok = by_device(usable)
    ordered_hot = by_device(picks == 0)
    onehot = jnp.where(ordered_ok[..., None], (ordered[..., None] == jnp.arange(NB, dtype=jnp.int32)).astype(jnp.int32), 0)
    slot_rank = jnp.sum((jnp.cumsum(onehot, axis=2) - 1) * onehot, axis=-1)
    limit = jnp.where(ordered_hot, CAP, CAP2)
    keeping = ordered_ok & (slot_rank < limit)
    keeping = keeping.reshape(dev_count, KVH, dev_rows, 2).transpose(0, 2, 1, 3).reshape(NQ, KVH, 2)
    chosen = jnp.where(keeping, picks, own_block[..., None])
    return jnp.concatenate([own_block[..., None], chosen], axis=-1).astype(jnp.int32)


def level_of(key, extent, shards, smallest, largest):
    level, own = 1.0, jax.random.fold_in(key, 6)
    for axis_at, blocks in shards:
        heights = jnp.exp(jax.random.uniform(jax.random.fold_in(own, axis_at), (blocks,), jnp.float32, smallest / len(shards), largest / len(shards)))
        level = level * jnp.repeat(heights, extent[axis_at] // blocks).reshape([-1 if axis == axis_at else 1 for axis in range(len(extent))])
    return level


def scatter_about(stream_key, shape, deviation, most, cuts=(), held_as=jnp.bfloat16):
    values = deviation * jax.random.normal(stream_key, shape, jnp.float32)
    if cuts:
        values = values * level_of(stream_key, shape, cuts, -0.22, 0.18)
    return jnp.clip(values, -most, most).astype(held_as)


def setup_inputs(seed: int = 0) -> dict:
    arg_keys = jax.random.split(jax.random.key(seed), 7)
    queries = draw_queries(jax.random.fold_in(arg_keys[6], 71), 0)
    keys = draw_keys(jax.random.fold_in(arg_keys[6], 71), 0)
    values = scatter_about(arg_keys[2], (SEQ, KVH * DH), 1.0, 5.0, ((0, 32), (1, 8)))
    grad_out = scatter_about(arg_keys[3], (NQ, HQ * DH), 1.0, 5.0, ((0, 256),))
    gates = draw_gates(jax.random.fold_in(arg_keys[6], 71), 0)
    block_order = draw_block_order(jax.random.fold_in(arg_keys[6], 71), 0)
    return {"queries": queries, "keys": keys, "values": values, "grad_out": grad_out, "gates": gates, "block_order": block_order}


NEG_FILL = -1.0e30


def reference(queries, keys, values, grad_out, gates, block_order):
    group_size = HQ // KVH
    softmax_scale = DH ** -0.5
    slot_of = jnp.zeros((NB,), jnp.int32).at[block_order].set(jnp.arange(NB, dtype=jnp.int32))
    key_blocks = keys.reshape(NB, BS, KVH, DH).transpose(0, 2, 1, 3)
    val_blocks = values.reshape(NB, BS, KVH, DH).transpose(0, 2, 1, 3)
    query_items = queries.reshape(NB, QB, KVH, group_size, DH)
    grad_items = grad_out.reshape(NB, QB, KVH, group_size, DH)
    gate_items = gates.reshape(NB, QB, KVH, 3)
    causal = jnp.arange(BS)[None, :] <= (BS - QB + jnp.arange(QB))[:, None]
    first_entry = (jnp.arange(3) == 0)[None, :, None]

    def one_item(item_id, state_acc):
        out_acc, dq_acc, dk_acc, dv_acc = state_acc
        slot_id = item_id // KVH
        head_id = item_id % KVH
        query_row_list = query_items[slot_id, :, head_id].astype(jnp.float32)
        gradient_row_list = grad_items[slot_id, :, head_id].astype(jnp.float32)
        chosen = gate_items[slot_id, :, head_id]
        present = (jnp.arange(3)[None, :] == 0) | (chosen != block_order[slot_id])
        target = slot_of[chosen]
        key_sel = key_blocks[target, head_id].astype(jnp.float32)
        val_sel = val_blocks[target, head_id].astype(jnp.float32)
        allowed = jnp.where(first_entry, causal[:, None, :], present[:, :, None])
        scores = jnp.einsum("rgd,rejd->rgej", query_row_list, key_sel) * softmax_scale
        scores = jnp.where(allowed[:, None], scores, NEG_FILL)
        top_score = jnp.max(scores, axis=-1, keepdims=True)
        weights = jnp.exp(scores - top_score)
        total_weight = jnp.sum(weights, axis=-1, keepdims=True)
        part_lse = (top_score + jnp.log(total_weight))[..., 0]
        part_lse = jnp.where(present[:, None, :], part_lse, NEG_FILL)
        probability_half = (weights / total_weight).astype(jnp.bfloat16).astype(jnp.float32)
        part_out = jnp.einsum("rgej,rejd->rged", probability_half, val_sel)
        top_lse = jnp.max(part_lse, axis=-1, keepdims=True)
        logsum = top_lse + jnp.log(jnp.sum(jnp.exp(part_lse - top_lse), axis=-1, keepdims=True))
        out_rows = jnp.sum(jnp.exp(part_lse - logsum)[..., None] * part_out, axis=2).astype(jnp.bfloat16)
        delta_row = jnp.sum(gradient_row_list * out_rows.astype(jnp.float32), axis=-1)
        gate_matrix = jnp.exp(scores - logsum[..., None])
        dv_part = jnp.einsum("rgej,rgd->rejd", gate_matrix.astype(jnp.bfloat16).astype(jnp.float32), gradient_row_list)
        dprob = jnp.einsum("rgd,rejd->rgej", gradient_row_list, val_sel)
        score_gradient = (gate_matrix * (dprob - delta_row[:, :, None, None])).astype(jnp.bfloat16).astype(jnp.float32)
        dk_part = jnp.einsum("rgej,rgd->rejd", score_gradient, query_row_list) * softmax_scale
        dq_part = (jnp.einsum("rgej,rejd->rged", score_gradient, key_sel) * softmax_scale).astype(jnp.bfloat16)
        dq_rows = jnp.sum(dq_part.astype(jnp.float32), axis=2).astype(jnp.bfloat16)
        out_acc = out_acc.at[slot_id, :, head_id].set(out_rows)
        dq_acc = dq_acc.at[slot_id, :, head_id].set(dq_rows)
        dk_acc = dk_acc.at[target, head_id].add(dk_part)
        dv_acc = dv_acc.at[target, head_id].add(dv_part)
        return out_acc, dq_acc, dk_acc, dv_acc

    start_state = (jnp.zeros((NB, QB, KVH, group_size, DH), jnp.bfloat16),
                   jnp.zeros((NB, QB, KVH, group_size, DH), jnp.bfloat16),
                   jnp.zeros((NB, KVH, BS, DH), jnp.float32),
                   jnp.zeros((NB, KVH, BS, DH), jnp.float32))
    out_acc, dq_acc, dk_acc, dv_acc = lax.fori_loop(0, NB * KVH, one_item, start_state)
    attn_out = out_acc.reshape(NQ, HQ * DH)
    grad_queries = dq_acc.reshape(NQ, HQ * DH)
    grad_keys = dk_acc.transpose(0, 2, 1, 3).reshape(SEQ, KVH * DH).astype(jnp.bfloat16)
    grad_values = dv_acc.transpose(0, 2, 1, 3).reshape(SEQ, KVH * DH).astype(jnp.bfloat16)
    return (attn_out, grad_queries, grad_keys, grad_values)
```

```python
import functools

import jax
import jax.numpy as jnp
from jax import lax
from jax.experimental import pallas as pl
from jax.experimental.pallas import tpu as pltpu
from jax.sharding import PartitionSpec as P

DH = 128
HQ = 32
KVH = 8
GROUP = HQ // KVH
WIDTH = GROUP * DH
BS = 1024
QB = 128
CAP = 16
NB = 32
SLOTS = NB * CAP
SIDE = 3 * WIDTH
BACK = SIDE + 128
SCALE = DH ** (-0.5)
NEG_FILL = -1e30
BF = jnp.bfloat16
F32 = jnp.float32
VMEM_LIMIT = 56 * 1024 * 1024


def dot(a, b):
    return jnp.dot(a, b, preferred_element_type=F32)


def dot_first(a, b):
    return lax.dot_general(a, b, (((0,), (0,)), ((), ())), preferred_element_type=F32)


def split3(x):
    high = x.astype(BF)
    rest = x - high.astype(F32)
    middle = rest.astype(BF)
    low = (rest - middle.astype(F32)).astype(BF)
    return high, middle, low


def call(kernel, out_shape, **kwargs):
    return pl.pallas_call(
        kernel,
        out_shape=out_shape,
        compiler_params=pltpu.CompilerParams(vmem_limit_bytes=VMEM_LIMIT),
        **kwargs,
    )


def shape(dims, dtype):
    return jax.ShapeDtypeStruct(dims, dtype)


def pack_kernel(q_ref, do_ref, out_ref):
    for head in range(KVH):
        columns = slice(head * WIDTH, (head + 1) * WIDTH)
        out_ref[head, :, :WIDTH] = q_ref[:, columns]
        out_ref[head, :, WIDTH:] = do_ref[:, columns]


def route_kernel(gate_ref, order_ref, first_ref, second_ref):
    gates = gate_ref[...]
    order = order_ref[...]
    own = gates[:, 0:1]
    hits = []
    for entry in (1, 2):
        gate = gates[:, entry : entry + 1]
        hits.append(((gate == order) & (gate != own)).astype(F32))
    row = lax.broadcasted_iota(jnp.int32, (QB, QB), 0)
    column = lax.broadcasted_iota(jnp.int32, (QB, QB), 1)
    before = (column < row).astype(BF)
    slot = lax.broadcasted_iota(jnp.int32, (QB, NB), 1).astype(F32)
    place = lax.broadcasted_iota(jnp.int32, (QB, SLOTS), 1)
    taken = jnp.zeros((1, NB), F32)
    for hit, out_ref in zip(hits, (first_ref, second_ref)):
        rank = dot(before, hit.astype(BF)) + taken
        taken = taken + jnp.sum(hit, axis=0, keepdims=True)
        found = jnp.sum(hit, axis=1, keepdims=True)
        position = jnp.sum(hit * (slot * CAP + rank), axis=1, keepdims=True)
        position = jnp.where(found > 0.5, position, -1.0).astype(jnp.int32)
        out_ref[...] = (place == position).astype(BF)


def gather_kernel(rows_ref, first_ref, second_ref, out_ref):
    pick = first_ref[...] + second_ref[...]
    out_ref[...] = dot_first(pick, rows_ref[...]).astype(BF)


def attend(q_t, do_t, key, value, both_t, allowed):
    scores = dot(key, q_t) * SCALE
    if allowed is not None:
        scores = jnp.where(allowed, scores, NEG_FILL)
    top = jnp.max(scores, axis=0, keepdims=True)
    weights = jnp.exp(scores - top)
    total = jnp.sum(weights, axis=0, keepdims=True)
    weights = weights * (1.0 / total)
    prob = weights.astype(BF)
    sums = dot(both_t, prob)
    out_t = sums[:DH]
    key_sum_t = sums[DH:] * SCALE
    delta = jnp.sum(out_t * do_t.astype(F32), axis=0, keepdims=True)
    moved = (weights * (dot(value, do_t) - delta)).astype(BF)
    grad_t = dot(both_t[DH:], moved) * SCALE
    return prob, moved, out_t, grad_t, key_sum_t, top + jnp.log(total), delta


def own_kernel(rows_ref, key_ref, value_ref, prob_ref, moved_ref, res_ref, both_ref):
    key, value = key_ref[...], value_ref[...]
    both_ref[:DH] = value.astype(F32).T.astype(BF)
    both_ref[DH:] = key.astype(F32).T.astype(BF)
    both_t = both_ref[...]
    rows_t = rows_ref[...].astype(F32).T.astype(BF)
    q_t = jnp.concatenate([rows_t[j * DH : (j + 1) * DH] for j in range(GROUP)], axis=1)
    do_t = jnp.concatenate([rows_t[WIDTH + j * DH : WIDTH + (j + 1) * DH] for j in range(GROUP)], axis=1)
    key_at = lax.broadcasted_iota(jnp.int32, (BS, WIDTH), 0)
    row_at = lax.broadcasted_iota(jnp.int32, (BS, WIDTH), 1) % QB
    allowed = key_at <= row_at + (BS - QB)
    prob, moved, out_t, grad_t, key_sum_t, lse, delta = attend(q_t, do_t, key, value, both_t, allowed)
    prob_ref[...] = prob
    moved_ref[...] = moved
    line = lax.broadcasted_iota(jnp.int32, (DH, QB), 0)
    side_t = jnp.zeros((DH, QB), F32)
    for j in range(GROUP):
        columns = slice(j * QB, (j + 1) * QB)
        for part, piece in enumerate((out_t, grad_t, key_sum_t)):
            res_ref[:, part * WIDTH + j * DH : part * WIDTH + (j + 1) * DH] = piece[:, columns].T
        side_t = jnp.where(line == j, lse[:, columns], side_t)
        side_t = jnp.where(line == GROUP + j, delta[:, columns], side_t)
    res_ref[:, SIDE:] = side_t.T


def far_kernel(q_ref, do_ref, key_ref, value_ref, both_ref, prob_ref, moved_ref, back_ref, side_ref):
    j = pl.program_id(0)
    q_t = q_ref[...].astype(F32).T.astype(BF)
    do_t = do_ref[...].astype(F32).T.astype(BF)
    prob, moved, out_t, grad_t, key_sum_t, lse, delta = attend(
        q_t, do_t, key_ref[...], value_ref[...], both_ref[...], None
    )
    prob_ref[...] = prob
    moved_ref[...] = moved
    for part, piece in enumerate((out_t, grad_t, key_sum_t)):
        at = pl.multiple_of(part * WIDTH + j * DH, DH)
        back_ref[:, pl.ds(at, DH)] = piece.T.astype(BF)
    line = lax.broadcasted_iota(jnp.int32, (DH, SLOTS), 0) - 8 * j
    side_t = jnp.zeros((DH, SLOTS), F32)
    for at, part in enumerate(split3(lse) + split3(delta)):
        side_t = jnp.where(line == at, part.astype(F32), side_t)

    @pl.when(j == 0)
    def _():
        side_ref[...] = side_t

    @pl.when(j > 0)
    def _():
        side_ref[...] += side_t

    @pl.when(j == GROUP - 1)
    def _():
        back_ref[:, SIDE:] = side_ref[...].T.astype(BF)


def combine_kernel(got_ref, first_ref, second_ref, own_ref, rows_ref, send_ref, stats_ref, scaled_ref):
    got = got_ref[...]
    picks = (first_ref[...], second_ref[...])
    far = [dot(pick, got) for pick in picks]
    there = [jnp.sum(pick.astype(F32), axis=1, keepdims=True) > 0.5 for pick in picks]
    lane = lax.broadcasted_iota(jnp.int32, (QB, 128), 1)
    tiled = [jnp.zeros((QB, 128), F32) for _ in picks]
    for j in range(GROUP):
        head = [slice(part * WIDTH + j * DH, part * WIDTH + (j + 1) * DH) for part in range(3)]
        side = own_ref[:, SIDE:]
        lses = [side[:, j : j + 1]]
        deltas = [side[:, GROUP + j : GROUP + j + 1]]
        for piece, here in zip(far, there):
            parts = piece[:, SIDE + 8 * j : SIDE + 8 * j + 6]
            lse = parts[:, 0:1] + parts[:, 1:2] + parts[:, 2:3]
            lses.append(jnp.where(here, lse, NEG_FILL))
            deltas.append(parts[:, 3:4] + parts[:, 4:5] + parts[:, 5:6])
        top = jnp.maximum(jnp.maximum(lses[0], lses[1]), lses[2])
        total = sum(jnp.exp(lse - top) for lse in lses)
        logsum = top + jnp.log(total)
        shares = [jnp.exp(lse - logsum) for lse in lses]
        pieces = [own_ref[...]] + far
        out = sum(share * piece[:, head[0]] for share, piece in zip(shares, pieces)).astype(BF)
        q = rows_ref[:, j * DH : (j + 1) * DH].astype(F32)
        do = rows_ref[:, WIDTH + j * DH : WIDTH + (j + 1) * DH].astype(F32)
        delta = jnp.sum(out.astype(F32) * do, axis=1, keepdims=True)
        moves = [share * (own - delta) for share, own in zip(shares, deltas)]
        grad = sum(
            share * piece[:, head[1]] + move * piece[:, head[2]]
            for share, move, piece in zip(shares, moves, pieces)
        )
        send_ref[:, j * DH : (j + 1) * DH] = out
        send_ref[:, WIDTH + j * DH : WIDTH + (j + 1) * DH] = grad.astype(BF)
        at = slice(j * QB, (j + 1) * QB)
        scaled_ref[at, :DH] = (shares[0] * do).astype(BF)
        scaled_ref[at, DH : 2 * DH] = (moves[0] * q).astype(BF)
        scaled_ref[at, 2 * DH :] = (shares[0] * q).astype(BF)
        for e in range(2):
            tiled[e] = jnp.where(lane % 8 == j, shares[e + 1], tiled[e])
            tiled[e] = jnp.where(lane % 8 == GROUP + j, moves[e + 1], tiled[e])
    spread = jnp.zeros((SLOTS, 128), F32)
    for pick, values in zip(picks, tiled):
        for part in split3(values):
            spread = spread + dot_first(pick, part)
    rank = lax.broadcasted_iota(jnp.int32, (SLOTS, 128), 0) % CAP
    keep = lax.broadcasted_iota(jnp.int32, (SLOTS, 128), 1) // 8 == rank
    stats_ref[...] = jnp.sum(jnp.where(keep, spread, 0.0).reshape(NB, CAP, 128), axis=1)


def grads_kernel(
    stats_ref, q_ref, do_ref, prob_ref, moved_ref, own_prob_ref, own_moved_ref, scaled_ref,
    grad_k_ref, grad_v_ref, share_ref, sum_ref,
):
    j = pl.program_id(0)
    lane = lax.broadcasted_iota(jnp.int32, (SLOTS, 128), 1)

    @pl.when(j == 0)
    def _():
        rank = lax.broadcasted_iota(jnp.int32, (SLOTS, 128), 0) % CAP
        wide = jnp.broadcast_to(stats_ref[...][:, None, :], (NB, CAP, 128)).reshape(SLOTS, 128)
        wide = jnp.where(lane // 8 == rank, wide, 0.0)
        for step in (8, 16, 32, 64):
            wide = wide + pltpu.roll(wide, step, 1)
        share_ref[...] = wide

    stats = share_ref[...]
    share = jnp.sum(jnp.where(lane == j, stats, 0.0), axis=1, keepdims=True)
    move = jnp.sum(jnp.where(lane == GROUP + j, stats, 0.0), axis=1, keepdims=True)
    q = q_ref[...].astype(F32)
    do = do_ref[...].astype(F32)
    pair = jnp.concatenate([(share * do).astype(BF), (move * q).astype(BF)], axis=1)
    scaled = scaled_ref[...]
    first = dot(prob_ref[...], pair) + dot(own_prob_ref[...], scaled[:, : 2 * DH])
    second = dot(moved_ref[...], (share * q).astype(BF)) + dot(own_moved_ref[...], scaled[:, 2 * DH :])
    both = jnp.concatenate([first[:, :DH], first[:, DH:] + second], axis=1)

    @pl.when(j == 0)
    def _():
        sum_ref[...] = both

    @pl.when(j > 0)
    def _():
        sum_ref[...] += both

    @pl.when(j == GROUP - 1)
    def _():
        grad_v_ref[...] = sum_ref[:, :DH].astype(BF)
        grad_k_ref[...] = (sum_ref[:, DH:] * SCALE).astype(BF)


def unpack_kernel(got_ref, out_ref, dq_ref):
    for head in range(KVH):
        columns = slice(head * WIDTH, (head + 1) * WIDTH)
        out_ref[:, columns] = got_ref[head, :, :WIDTH]
        dq_ref[:, columns] = got_ref[head, :, WIDTH:]


def exchange(array, axis):
    return lax.all_to_all(array, axis, split_axis=0, concat_axis=0, tiled=True)


def on_device(queries, keys, values, grad_out, gates, block_order):
    packed = call(pack_kernel, shape((KVH, QB // KVH, 2 * WIDTH), BF))(queries, grad_out)
    first, second = call(route_kernel, [shape((QB, SLOTS), BF)] * 2)(
        gates.reshape(QB, 3), block_order.reshape(1, NB)
    )
    rows = exchange(packed, "head").reshape(QB, 2 * WIDTH)
    sent = call(gather_kernel, shape((SLOTS, 2 * WIDTH), BF))(rows, first, second)
    got = exchange(sent.reshape(NB, CAP, 2 * WIDTH), "ctx").reshape(SLOTS, 2 * WIDTH)
    own_prob, own_moved, own_res, both_t = call(
        own_kernel,
        [
            shape((BS, WIDTH), BF),
            shape((BS, WIDTH), BF),
            shape((QB, BACK), F32),
            shape((2 * DH, BS), BF),
        ],
    )(rows, keys, values)
    whole = lambda *dims: pl.BlockSpec(dims, lambda j: (0,) * len(dims))
    query_spec = pl.BlockSpec((SLOTS, DH), lambda j: (0, j))
    grad_spec = pl.BlockSpec((SLOTS, DH), lambda j: (0, GROUP + j))
    tall = lambda columns: pl.BlockSpec((BS, columns), lambda j: (0, j))
    prob, moved, back = call(
        far_kernel,
        [shape((BS, GROUP * SLOTS), BF), shape((BS, GROUP * SLOTS), BF), shape((SLOTS, BACK), BF)],
        grid=(GROUP,),
        in_specs=[query_spec, grad_spec, whole(BS, DH), whole(BS, DH), whole(2 * DH, BS)],
        out_specs=[tall(SLOTS), tall(SLOTS), whole(SLOTS, BACK)],
        scratch_shapes=[pltpu.VMEM((DH, SLOTS), F32)],
    )(got, got, keys, values, both_t)
    returned = exchange(back.reshape(NB, CAP, BACK), "ctx").reshape(SLOTS, BACK)
    send, stats, scaled = call(
        combine_kernel,
        [shape((QB, 2 * WIDTH), BF), shape((NB, 128), F32), shape((GROUP * QB, 3 * DH), BF)],
    )(returned, first, second, own_res, rows)
    stats_got = exchange(stats.reshape(NB, 1, 128), "ctx").reshape(NB, 128)
    tokens = exchange(send.reshape(KVH, QB // KVH, 2 * WIDTH), "head")
    grad_keys, grad_values = call(
        grads_kernel,
        [shape((BS, DH), BF), shape((BS, DH), BF)],
        grid=(GROUP,),
        in_specs=[
            whole(NB, 128),
            query_spec,
            grad_spec,
            tall(SLOTS),
            tall(SLOTS),
            tall(QB),
            tall(QB),
            pl.BlockSpec((QB, 3 * DH), lambda j: (j, 0)),
        ],
        out_specs=[whole(BS, DH), whole(BS, DH)],
        scratch_shapes=[pltpu.VMEM((SLOTS, 128), F32), pltpu.VMEM((BS, 2 * DH), F32)],
    )(stats_got, got, got, prob, moved, own_prob, own_moved, scaled)
    attn_out, grad_queries = call(unpack_kernel, [shape((QB // KVH, HQ * DH), BF)] * 2)(tokens)
    return attn_out, grad_queries, grad_keys, grad_values


def solution(mesh):
    return jax.shard_map(
        on_device,
        mesh=mesh,
        in_specs=(
            P(("ctx", "head"), None),
            P("ctx", "head"),
            P("ctx", "head"),
            P(("ctx", "head"), None),
            P("ctx", "head", None),
            P(),
        ),
        out_specs=(
            P(("ctx", "head"), None),
            P(("ctx", "head"), None),
            P("ctx", "head"),
            P("ctx", "head"),
        ),
        check_vma=False,
    )
```
